32 devices in a mesh: groups: 2 (over y), ep: 4 (over z), tp: 4 (over x, core).
Axes of the slice: x: 2, y: 2, z: 4, core: 2. Of those that a mesh axis runs over, the one named last changes fastest.
Arguments:
- x_rows: bfloat16 [128, 4096], P(('groups', 'ep', 'tp')), parts along dimension 0, may hold values from -6 to 6
- queries: bfloat16 [128, 4096], P(('groups', 'ep', 'tp')), parts along dimension 0, may hold values from -80 to 80
- key_cache: bfloat16 [128, 64, 256], P(('groups', 'ep', 'tp')), parts along dimension 0, may hold values from -4 to 4
- value_cache: bfloat16 [128, 64, 256], P(('groups', 'ep', 'tp')), parts along dimension 0, may hold values from -6 to 6
- new_key: bfloat16 [128, 256], P(('groups', 'ep', 'tp')), parts along dimension 0, may hold values from -4 to 4
- new_value: bfloat16 [128, 256], P(('groups', 'ep', 'tp')), parts along dimension 0, may hold values from -6 to 6
- lengths: int32 [128], P(('groups', 'ep', 'tp')), parts along dimension 0, may hold values from 2 to 64, as said below
- norm_gain: bfloat16 [4096], replicated, may hold values from 0.099609375 to 1.8984375
- expert_ids: int32 [128, 8], P(('groups', 'ep', 'tp')), parts along dimension 0, may hold values from 0 to 15, all different within a row; in each aligned block of 4 rows (0 to 3, 4 to 7, ...) at most 4 rows name the same one
- gate_probs: float32 [128, 8], P(('groups', 'ep', 'tp')), parts along dimension 0, may hold values from 0.02 to 0.4
- expert_place: int32 [16], replicated, may hold values from 0 to 15, each once
- w_gate: bfloat16 [16, 4096, 1536], P('ep', None, 'tp'), may hold values from -0.09375 to 0.09375
- w_up: bfloat16 [16, 4096, 1536], P('ep', None, 'tp'), may hold values from -0.09375 to 0.09375
- w_down: bfloat16 [16, 1536, 4096], P('ep', 'tp'), may hold values from -0.15625 to 0.15625
Outputs:
- layer_out: bfloat16 [128, 4096], P(('groups', 'ep', 'tp')), parts along dimension 0
- expert_mix: bfloat16 [128, 4096], P(('groups', 'ep', 'tp')), parts along dimension 0
The draws below stay inside these ranges and needn't reach their ends.
There are 2 independent parts, one for each index of `groups`. The reference program is written for one: setup_inputs(seed, part) draws one part's arguments, and reference() takes and returns one part's arrays. A program takes and returns all parts, laid end to end along the dimension named above; an argument that names none is the same for every part. Nothing has to cross between parts.
Inputs may be any that keep to these rules, and one draw needn't show every extreme that they name: `expert_ids`: each row names 8 different experts; among the 4 rows of one device no expert is named more than 4 times. `expert_place`: a permutation; slot j lies on index j // 4 of ep. `lengths`: some request has exactly 64 positions.
All inputs are finite; a program needn't handle non-finite values.
Results may differ from the reference program's by a relative error of at most 0.012.
Values may be sent and summed in bfloat16 or wider, within the bound.
A program may use at most 128 MiB of HBM per device.

```python
import math
import jax
import jax.numpy as jnp
import numpy as np
from jax import lax

D = 4096
FF = 1536
HEAD_DIM = 128
TOP = 8
Q_HEADS = 32
KV_HEADS = 2
TOK_DEV = 4
LMAX = 64
EXPERTS = 16
MOST = 4
TOKENS = 64
N_EP = 4
N_TP = 4


def cache_base(key):
    base = jax.random.normal(jax.random.fold_in(key, 101), (TOKENS, LMAX, KV_HEADS * HEAD_DIM), jnp.float32)
    return jnp.clip(base, -4.0, 4.0)


def draw_key_cache(key, part):
    shared = cache_base(key)
    return shared.astype(jnp.bfloat16)


def draw_queries(key, part):
    key = jax.random.fold_in(key, 2)
    drawn = jnp.clip(jax.random.normal(jax.random.fold_in(key, 7), (TOKENS, Q_HEADS * HEAD_DIM), jnp.float32), -4.0, 4.0)
    return drawn.astype(jnp.bfloat16)


def draw_lengths(key, part):
    key = jax.random.fold_in(key, 3)
    spans = jax.random.randint(jax.random.fold_in(key, 1), (TOKENS,), 2, LMAX + 1)
    longest = jax.random.randint(jax.random.fold_in(key, 2), (), 0, TOKENS)
    return spans.at[longest].set(LMAX).astype(jnp.int32)


def shard_levels(rng, shape, cuts, low, largest):
    level, own = 1.0, jax.random.fold_in(rng, 6)
    for dim, parts in cuts:
        steps = jnp.exp(jax.random.uniform(jax.random.fold_in(own, dim), (parts,), jnp.float32, low / len(cuts), largest / len(cuts)))
        level = level * jnp.repeat(steps, shape[dim] // parts).reshape([-1 if axis == dim else 1 for axis in range(len(shape))])
    return level


def assign_block(own_key, own, number, rows, number_of, top, bound, lean):
    ranking = jax.random.permutation(own_key, number_of)
    heavy_load, usual = shares(number_of, rows * top, bound, lean, True), shares(number_of, rows * top, bound, lean, False)
    places = jnp.arange(number_of)

    def named(sizes, rotation):
        used = int((sizes > 0).sum())
        fixed = max(1, used // 4)
        shifted = fixed + (places - fixed + rotation * (used - fixed)) % max(1, number_of - fixed)
        return jnp.zeros((number_of,), jnp.int32).at[ranking[jnp.where(places < fixed, places, shifted)]].set(jnp.asarray(sizes, jnp.int32))

    sizes = jnp.where(number % 4 == 0, named(heavy_load, number // 4), named(usual, number - number // 4 - 1))
    mixed = jax.random.permutation(jax.random.fold_in(own, 3), number_of)
    giver, taker = mixed[0:number_of // 2 * 2:2], mixed[1:number_of // 2 * 2:2]
    margin = jnp.minimum(sizes[giver] - 1, bound - sizes[taker]) // 2
    margin = jnp.where((giver == ranking[0]) | (taker == ranking[0]) | (sizes[taker] == 0), 0, jnp.maximum(margin, 0))
    shifted = jax.random.randint(jax.random.fold_in(own, 4), (number_of // 2,), 0, 1 << 20) % (margin + 1)
    sizes = sizes.at[giver].add(-shifted).at[taker].add(shifted)
    items = jnp.searchsorted(jnp.cumsum(sizes), jnp.arange(rows * top), side="right").astype(jnp.int32)
    listing = items.reshape(top, rows).T
    listing = listing[jax.random.permutation(jax.random.fold_in(own, 1), rows)]
    rotation = jax.random.randint(jax.random.fold_in(own, 2), (rows, 1), 0, top)
    return jnp.take_along_axis(listing, (jnp.arange(top)[None, :] + rotation) % top, axis=1)


def shares(amount, total, bound, skew, full):
    portions = [(1 << 20) // math.isqrt(rank ** skew) + 1 for rank in range(1, amount + 1)]
    largest = bound if full else min(bound, max(-(-total // amount), total * portions[0] // sum(portions)))
    least = 1 if total - largest >= amount - 1 else 0
    counts, surplus = [largest] + [least] * (amount - 1), total - largest - least * (amount - 1)
    while surplus > 0:
        movable = [i for i in range(1, amount) if counts[i] < largest] or [i for i in range(1, amount) if counts[i] < bound]
        pool, remaining = sum([portions[i] for i in movable]), surplus
        for i in movable:
            extra = min(bound - counts[i], max(1, remaining * portions[i] // pool), surplus)
            counts[i] = counts[i] + extra
            surplus = surplus - extra
    return np.array(counts)


def gaussian(own_key, shape, spread, bound, shards=(), kind=jnp.bfloat16):
    entries = jax.random.normal(own_key, shape, jnp.float32) * spread
    if len(shards) > 0:
        entries = shard_levels(own_key, shape, shards, -0.22, 0.18) * entries
    return jnp.clip(entries, min=-bound, max=bound).astype(kind)


def setup_inputs(seed: int = 0, part: int = 0) -> dict:
    streams_of = jax.random.split(jax.random.key(seed), 15)
    own_keys = jax.random.split(jax.random.fold_in(streams_of[14], part), 15)
    x_rows = gaussian(own_keys[0], (TOKENS, D), 1.0, 6.0, ((0, 16),))
    queries = draw_queries(jax.random.fold_in(jax.random.fold_in(streams_of[14], part), 71), part)
    key_cache = draw_key_cache(jax.random.fold_in(jax.random.fold_in(streams_of[14], part), 71), part)
    value_cache = gaussian(own_keys[3], (TOKENS, LMAX, KV_HEADS * HEAD_DIM), 1.0, 6.0, ((0, 16),))
    new_key = gaussian(own_keys[4], (TOKENS, KV_HEADS * HEAD_DIM), 1.0, 4.0, ((0, 16),))
    new_value = gaussian(own_keys[5], (TOKENS, KV_HEADS * HEAD_DIM), 1.0, 6.0, ((0, 16),))
    lengths = draw_lengths(jax.random.fold_in(jax.random.fold_in(streams_of[14], part), 71), part)
    norm_gain = jnp.clip(1.0 + 0.18 * jax.random.normal(streams_of[7], (D,), jnp.float32), 0.099609375, 1.8984375).astype(jnp.bfloat16)
    expert_ids_keys = jax.random.split(jax.random.fold_in(own_keys[8], 1), TOKENS // TOK_DEV)
    expert_ids_turns = jax.random.permutation(jax.random.fold_in(own_keys[8], 3), TOKENS // TOK_DEV)
    expert_ids = jax.vmap(lambda own, number: assign_block(jax.random.fold_in(own_keys[8], 2), own, number, TOK_DEV, EXPERTS, TOP, MOST, 2))(expert_ids_keys, expert_ids_turns).reshape((TOKENS, TOP))
    gate_probs = jnp.clip(jnp.exp(math.log(0.4) - 2.9957323 * jax.random.uniform(own_keys[9], (TOKENS, TOP), jnp.float32) ** shard_levels(own_keys[9], (TOKENS, TOP), ((0, 16),), -0.2, 0.2)), 0.02, 0.4)
    expert_place = jax.random.permutation(streams_of[10], EXPERTS).astype(jnp.int32)
    w_gate = gaussian(streams_of[11], (EXPERTS, D, FF), D ** -0.5, 0.09375, ((0, 4), (2, 4)))
    w_up = gaussian(streams_of[12], (EXPERTS, D, FF), D ** -0.5, 0.09375, ((0, 4), (2, 4)))
    w_down = gaussian(streams_of[13], (EXPERTS, FF, D), FF ** -0.5, 0.15625, ((0, 4), (1, 4)))
    return dict(x_rows=x_rows, queries=queries, key_cache=key_cache, value_cache=value_cache, new_key=new_key, new_value=new_value, lengths=lengths, norm_gain=norm_gain, expert_ids=expert_ids, gate_probs=gate_probs, expert_place=expert_place, w_gate=w_gate, w_up=w_up, w_down=w_down)


highest = lax.Precision.HIGHEST

def attend(queries, key_cache, value_cache, new_key, new_value, lengths):
    row_count = queries.shape[0]
    span = key_cache.shape[1]
    groups = Q_HEADS // KV_HEADS
    factor = HEAD_DIM ** (-0.5)
    query = queries.astype(jnp.float32).reshape(row_count, KV_HEADS, groups, HEAD_DIM)
    cached_keys = key_cache.astype(jnp.float32).reshape(row_count, span, KV_HEADS, HEAD_DIM)
    cached_values = value_cache.astype(jnp.float32).reshape(row_count, span, KV_HEADS, HEAD_DIM)
    fresh_key = new_key.astype(jnp.float32).reshape(row_count, KV_HEADS, HEAD_DIM)
    fresh_value = new_value.astype(jnp.float32).reshape(row_count, KV_HEADS, HEAD_DIM)
    scores = jnp.einsum('rgjd,rpgd->rgjp', query, cached_keys, precision=highest) * factor
    own_score = jnp.einsum('rgjd,rgd->rgj', query, fresh_key, precision=highest) * factor
    valid = (jnp.arange(span, dtype=jnp.int32)[None, :] < lengths[:, None])[:, None, None, :]
    masked = jnp.where(valid, scores, -1e+30)
    peak_all = jnp.maximum(lax.optimization_barrier(jnp.max(masked, axis=3)), own_score)
    weights = jnp.where(valid, jnp.exp(masked - peak_all[..., None]), 0.0)
    own_weight = jnp.exp(own_score - peak_all)
    denominator = lax.optimization_barrier(jnp.sum(weights, axis=3)) + own_weight
    summed = jnp.einsum('rgjp,rpgd->rgjd', weights, cached_values, precision=highest)
    summed = summed + own_weight[..., None] * fresh_value[:, :, None, :]
    return (summed / denominator[..., None]).reshape(row_count, Q_HEADS * HEAD_DIM)

def reference(x_rows, queries, key_cache, value_cache, new_key, new_value, lengths, norm_gain, expert_ids, gate_probs, expert_place, w_gate, w_up, w_down):
    stream = x_rows.astype(jnp.float32) + attend(queries, key_cache, value_cache, new_key, new_value, lengths)
    scaled = lax.rsqrt(lax.optimization_barrier(jnp.mean(stream * stream, axis=1, keepdims=True)) + 1e-06)
    normed = (stream * scaled * norm_gain.astype(jnp.float32)).astype(jnp.bfloat16)
    target = expert_place[expert_ids].reshape(-1).astype(jnp.int32)
    weight_flat = jnp.concatenate([gate_probs.reshape(-1), jnp.zeros((1,), jnp.float32)])
    padded = jnp.concatenate([normed, jnp.zeros((1, D), jnp.bfloat16)], axis=0)
    block = FF // N_TP
    capacity = N_EP * N_TP * MOST

    def one_expert(running, item):
        gate_w, up_w, down_w, index = item
        chosen = jnp.nonzero(target == index, size=capacity, fill_value=TOKENS * TOP)[0].astype(jnp.int32)
        token_of = chosen // TOP
        rows_in = padded[token_of]
        gate_act = jnp.dot(rows_in, gate_w, preferred_element_type=jnp.float32)
        up_act = jnp.dot(rows_in, up_w, preferred_element_type=jnp.float32)
        hidden = (jax.nn.silu(gate_act) * up_act).astype(jnp.bfloat16)
        result = jnp.zeros((capacity, D), jnp.float32)
        for piece_index in range(N_TP):
            lower = piece_index * block
            term = jnp.dot(hidden[:, lower:lower + block], down_w[lower:lower + block], preferred_element_type=jnp.float32).astype(jnp.bfloat16)
            result = result + lax.optimization_barrier(term).astype(jnp.float32)
        running = running.at[token_of].add(weight_flat[chosen][:, None] * result)
        return (running, None)
    mixed, _ = lax.scan(one_expert, jnp.zeros((TOKENS + 1, D), jnp.float32), (w_gate, w_up, w_down, jnp.arange(EXPERTS, dtype=jnp.int32)))
    mixed = mixed[:TOKENS]
    return ((stream + mixed).astype(jnp.bfloat16), mixed.astype(jnp.bfloat16))
```

```python
import jax
import jax.numpy as jnp
from jax import lax
from jax.sharding import PartitionSpec as P

HEAD_DIM = 128
Q_HEADS = 32
KV_HEADS = 2


highest = lax.Precision.HIGHEST


def attend(queries, key_cache, value_cache, new_key, new_value, lengths):
    row_count = queries.shape[0]
    span = key_cache.shape[1]
    groups = Q_HEADS // KV_HEADS
    factor = HEAD_DIM ** (-0.5)
    query = queries.astype(jnp.float32).reshape(row_count, KV_HEADS, groups, HEAD_DIM)
    cached_keys = key_cache.astype(jnp.float32).reshape(row_count, span, KV_HEADS, HEAD_DIM)
    cached_values = value_cache.astype(jnp.float32).reshape(row_count, span, KV_HEADS, HEAD_DIM)
    fresh_key = new_key.astype(jnp.float32).reshape(row_count, KV_HEADS, HEAD_DIM)
    fresh_value = new_value.astype(jnp.float32).reshape(row_count, KV_HEADS, HEAD_DIM)
    scores = jnp.einsum("rgjd,rpgd->rgjp", query, cached_keys, precision=highest) * factor
    own_score = jnp.einsum("rgjd,rgd->rgj", query, fresh_key, precision=highest) * factor
    valid = (jnp.arange(span, dtype=jnp.int32)[None, :] < lengths[:, None])[:, None, None, :]
    masked = jnp.where(valid, scores, -1e30)
    peak_all = jnp.maximum(jnp.max(masked, axis=3), own_score)
    weights = jnp.where(valid, jnp.exp(masked - peak_all[..., None]), 0.0)
    own_weight = jnp.exp(own_score - peak_all)
    denominator = jnp.sum(weights, axis=3) + own_weight
    summed = jnp.einsum("rgjp,rpgd->rgjd", weights, cached_values, precision=highest)
    summed = summed + own_weight[..., None] * fresh_value[:, :, None, :]
    return (summed / denominator[..., None]).reshape(row_count, Q_HEADS * HEAD_DIM)


def local(
    x_rows,
    queries,
    key_cache,
    value_cache,
    new_key,
    new_value,
    lengths,
    norm_gain,
    expert_ids,
    gate_probs,
    expert_place,
    w_gate,
    w_up,
    w_down,
):
    row_count = x_rows.shape[0]
    width = x_rows.shape[1]
    stream = x_rows.astype(jnp.float32) + attend(
        queries, key_cache, value_cache, new_key, new_value, lengths
    )
    scaled = lax.rsqrt(jnp.mean(stream * stream, axis=1, keepdims=True) + 1e-06)
    normed = (stream * scaled * norm_gain.astype(jnp.float32)).astype(jnp.bfloat16)
    experts_total = expert_place.shape[0]
    local_experts = w_gate.shape[0]
    expert_range = jnp.arange(experts_total, dtype=jnp.int32)
    target = jnp.sum(jnp.where(expert_ids[:, :, None] == expert_range, expert_place, 0), axis=2)
    table = jnp.sum(
        jnp.where(target[:, :, None] == expert_range, gate_probs[:, :, None], 0.0), axis=1
    )
    high = lax.reduce_precision(table, 8, 7)
    middle = lax.reduce_precision(table - high, 8, 7)
    low = table - high - middle
    pad = (-3 * experts_total) % 128
    pieces = jnp.concatenate(
        [high, middle, low, jnp.zeros((row_count, pad), jnp.float32)], axis=1
    ).astype(jnp.bfloat16)
    gathered = lax.all_gather(
        jnp.concatenate([normed, pieces], axis=1), ("ep", "tp"), axis=0, tiled=True
    )
    rows = gathered[:, :width]
    sent = gathered[:, width : width + 3 * experts_total].astype(jnp.float32)
    first = lax.axis_index("ep") * local_experts
    parts = sent.reshape(-1, 3, experts_total)
    weights = lax.dynamic_slice_in_dim(
        parts[:, 0] + (parts[:, 1] + parts[:, 2]), first, local_experts, axis=1
    )
    gate_act = jnp.einsum("sd,edf->esf", rows, w_gate, preferred_element_type=jnp.float32)
    up_act = jnp.einsum("sd,edf->esf", rows, w_up, preferred_element_type=jnp.float32)
    hidden = (jax.nn.silu(gate_act) * up_act * weights.T[:, :, None]).astype(jnp.bfloat16)
    partial_value = jnp.einsum(
        "esf,efd->sd", hidden, w_down, preferred_element_type=jnp.float32
    ).astype(jnp.bfloat16)
    mixed = lax.psum_scatter(
        partial_value, ("ep", "tp"), scatter_dimension=0, tiled=True
    ).astype(jnp.float32)
    return ((stream + mixed).astype(jnp.bfloat16), mixed.astype(jnp.bfloat16))


def solution(mesh):
    return jax.shard_map(
        local,
        mesh=mesh,
        in_specs=(
            P(("groups", "ep", "tp"), None),
            P(("groups", "ep", "tp"), None),
            P(("groups", "ep", "tp"), None, None),
            P(("groups", "ep", "tp"), None, None),
            P(("groups", "ep", "tp"), None),
            P(("groups", "ep", "tp"), None),
            P(("groups", "ep", "tp")),
            P(),
            P(("groups", "ep", "tp"), None),
            P(("groups", "ep", "tp"), None),
            P(),
            P("ep", None, "tp"),
            P("ep", None, "tp"),
            P("ep", "tp", None),
        ),
        out_specs=(P(("groups", "ep", "tp"), None), P(("groups", "ep", "tp"), None)),
        check_vma=False,
    )
```

```python
import functools

import jax
import jax.numpy as jnp
from jax import lax
from jax.experimental import pallas as pl
from jax.experimental.pallas import tpu as pltpu
from jax.sharding import PartitionSpec as P

HEAD_DIM = 128
Q_HEADS = 32
KV_HEADS = 2


highest = lax.Precision.HIGHEST


def attend(queries, key_cache, value_cache, new_key, new_value, lengths):
    row_count = queries.shape[0]
    span = key_cache.shape[1]
    groups = Q_HEADS // KV_HEADS
    factor = HEAD_DIM ** (-0.5)
    query = queries.astype(jnp.float32).reshape(row_count, KV_HEADS, groups, HEAD_DIM)
    cached_keys = key_cache.astype(jnp.float32).reshape(row_count, span, KV_HEADS, HEAD_DIM)
    cached_values = value_cache.astype(jnp.float32).reshape(row_count, span, KV_HEADS, HEAD_DIM)
    fresh_key = new_key.astype(jnp.float32).reshape(row_count, KV_HEADS, HEAD_DIM)
    fresh_value = new_value.astype(jnp.float32).reshape(row_count, KV_HEADS, HEAD_DIM)
    scores = jnp.einsum("rgjd,rpgd->rgjp", query, cached_keys, precision=highest) * factor
    own_score = jnp.einsum("rgjd,rgd->rgj", query, fresh_key, precision=highest) * factor
    valid = (jnp.arange(span, dtype=jnp.int32)[None, :] < lengths[:, None])[:, None, None, :]
    masked = jnp.where(valid, scores, -1e30)
    peak_all = jnp.maximum(jnp.max(masked, axis=3), own_score)
    weights = jnp.where(valid, jnp.exp(masked - peak_all[..., None]), 0.0)
    own_weight = jnp.exp(own_score - peak_all)
    denominator = jnp.sum(weights, axis=3) + own_weight
    summed = jnp.einsum("rgjp,rpgd->rgjd", weights, cached_values, precision=highest)
    summed = summed + own_weight[..., None] * fresh_value[:, :, None, :]
    return (summed / denominator[..., None]).reshape(row_count, Q_HEADS * HEAD_DIM)


CHUNKS = 4
MESH = pl.DeviceIdType.MESH


def flip(index, bit):
    return index + bit - 2 * bit * lax.rem(lax.div(index, bit), 2)


def low_bit(number):
    return number & -number


def experts_kernel(
    n_ep,
    n_tp,
    message_ref,
    stream_ref,
    w_gate,
    w_up,
    w_down,
    out_ref,
    mix_ref,
    gate_v,
    up_v,
    down_v,
    arrived,
    rows,
    hidden,
    sums,
    sent,
    taken,
    packed_wide,
    packed,
    back,
    weight_sem,
    ep_send,
    ep_recv,
    tp_send,
    tp_recv,
    sum_send,
    sum_recv,
    back_send,
    back_recv,
):
    experts, width, units = gate_v.shape
    row_count = stream_ref.shape[0]
    block = n_ep * row_count
    part = width // row_count
    span = width // CHUNKS
    piece = span // row_count
    bits = []
    bit = n_tp // 2
    while bit:
        bits.append(bit)
        bit //= 2
    me_ep = lax.axis_index("ep")
    me_tp = lax.axis_index("tp")

    loads = []
    for e in range(experts):
        for k, (source, target) in enumerate(((w_gate, gate_v), (w_up, up_v))):
            loads.append(
                pltpu.make_async_copy(source.at[e], target.at[e], weight_sem.at[2 * e + k])
            )
    down_load = pltpu.make_async_copy(w_down, down_v, weight_sem.at[2 * experts])
    for load in loads:
        load.start()
    down_load.start()

    arrived[0, 0] = message_ref[...]
    barrier = pltpu.get_barrier_semaphore()
    for j in range(1, n_ep):
        pl.semaphore_signal(
            barrier, inc=1, device_id={"ep": lax.rem(me_ep + j, n_ep)}, device_id_type=MESH
        )
    for b in bits:
        pl.semaphore_signal(barrier, inc=1, device_id={"tp": flip(me_tp, b)}, device_id_type=MESH)
    pl.semaphore_wait(barrier, n_ep - 1 + len(bits))

    sends = []
    along = {}
    for j in range(1, n_ep):
        s = n_ep - j
        along[s] = pltpu.make_async_remote_copy(
            src_ref=arrived.at[0, 0],
            dst_ref=arrived.at[0, s],
            send_sem=ep_send.at[s],
            recv_sem=ep_recv.at[s],
            device_id={"ep": lax.rem(me_ep + j, n_ep)},
            device_id_type=MESH,
        )
        along[s].start()
        sends.append(along[s])
    across = {}
    order = [0] + [s for d in range(1, n_ep) for s in (d, n_ep - d) if d <= s]
    order = list(dict.fromkeys(order))
    for m in range(n_tp):
        for s in order:
            if m:
                across[m, s].wait_recv()
            elif s:
                along[s].wait_recv()
            for b in bits:
                if m == 0 or b < low_bit(m):
                    copy = pltpu.make_async_remote_copy(
                        src_ref=arrived.at[m, s],
                        dst_ref=arrived.at[m | b, s],
                        send_sem=tp_send.at[m | b, s],
                        recv_sem=tp_recv.at[m | b, s],
                        device_id={"tp": flip(me_tp, b)},
                        device_id_type=MESH,
                    )
                    copy.start()
                    across[m | b, s] = copy
                    sends.append(copy)

    group = row_count * row_count
    to = lax.broadcasted_iota(jnp.int32, (block, n_ep * group), 0)
    source = lax.broadcasted_iota(jnp.int32, (block, n_ep * group), 1)
    tables = []
    for m in range(n_tp):
        held = arrived[m].reshape(n_ep * group, part + 128)
        table = jnp.zeros((block, 128), jnp.float32)
        for q in range(row_count):
            wanted = lax.div(to, row_count) * group + q * row_count + lax.rem(to, row_count)
            pick = jnp.where(source == wanted, 1.0, 0.0).astype(jnp.bfloat16)
            moved = jnp.dot(pick, held, preferred_element_type=jnp.float32)
            rows[m * block : (m + 1) * block, q * part : (q + 1) * part] = moved[:, :part].astype(
                jnp.bfloat16
            )
            table = table + moved[:, part:]
        tables.append(table)
    table = jnp.concatenate(tables, axis=0)
    lane = lax.broadcasted_iota(jnp.int32, table.shape, 1)

    for e in range(experts):
        loads[2 * e].wait()
        gate = jnp.dot(rows[...], gate_v[e], preferred_element_type=jnp.float32)
        loads[2 * e + 1].wait()
        up = jnp.dot(rows[...], up_v[e], preferred_element_type=jnp.float32)
        share = jnp.sum(
            jnp.where(lane == me_ep * experts + e, table, 0.0), axis=1, keepdims=True
        )
        act = gate / (1.0 + jnp.exp(-gate)) * up * share
        hidden[:, e * units : (e + 1) * units] = act.astype(jnp.bfloat16)
    down_load.wait()

    summing = {}
    returning = {}

    def columns(c):
        return slice(c * span, (c + 1) * span)

    def send_sums(c, b):
        for m in range(1, n_tp):
            if low_bit(m) == b:
                if b > 1:
                    sent[c, m] = sums[m // 2, :, columns(c)].astype(jnp.bfloat16)
                copy = pltpu.make_async_remote_copy(
                    src_ref=sent.at[c, m],
                    dst_ref=taken.at[c, m],
                    send_sem=sum_send.at[c, m],
                    recv_sem=sum_recv.at[c, m],
                    device_id={"tp": flip(me_tp, b)},
                    device_id_type=MESH,
                )
                copy.start()
                summing[c, m] = copy
                sends.append(copy)

    def take_sums(c, b):
        for m in range(1, n_tp):
            if low_bit(m) == b:
                summing[c, m].wait_recv()
                sums[(m - b) // 2, :, columns(c)] += taken[c, m].astype(jnp.float32)

    def send_back(c):
        for s in range(n_ep):
            for q in range(row_count):
                packed_wide[c, s, q * row_count : (q + 1) * row_count, :] = sums[
                    0,
                    s * row_count : (s + 1) * row_count,
                    c * span + q * piece : c * span + (q + 1) * piece,
                ]
            if s:
                packed[c, s] = packed_wide[c, s].astype(jnp.bfloat16)
                copy = pltpu.make_async_remote_copy(
                    src_ref=packed.at[c, s],
                    dst_ref=back.at[c, n_ep - s],
                    send_sem=back_send.at[c, n_ep - s],
                    recv_sem=back_recv.at[c, n_ep - s],
                    device_id={"ep": lax.rem(me_ep + s, n_ep)},
                    device_id_type=MESH,
                )
                copy.start()
                returning[c, s] = copy
                sends.append(copy)

    def compute(c):
        product = jnp.dot(hidden[...], down_v[:, columns(c)], preferred_element_type=jnp.float32)
        for m in range(n_tp):
            mine = product[m * block : (m + 1) * block]
            if m % 2:
                sent[c, m] = mine.astype(jnp.bfloat16)
            else:
                sums[m // 2, :, columns(c)] = mine
        if bits:
            send_sums(c, 1)
        else:
            send_back(c)

    def turn(c, k):
        b = 1 << k
        take_sums(c, b)
        if 2 * b < n_tp:
            send_sums(c, 2 * b)
        else:
            send_back(c)

    def finish(c):
        total = packed_wide[c, 0]
        for s in range(1, n_ep):
            returning[c, s].wait_recv()
            total = total + back[c, n_ep - s].astype(jnp.float32)
        packed_wide[c, 0] = total
        for q in range(row_count):
            place = slice(c * span + q * piece, c * span + (q + 1) * piece)
            mixed = packed_wide[c, 0, q * row_count : (q + 1) * row_count, :]
            mix_ref[:, place] = mixed.astype(jnp.bfloat16)
            out_ref[:, place] = (stream_ref[:, place] + mixed).astype(jnp.bfloat16)

    stages = [compute] + [functools.partial(turn, k=k) for k in range(len(bits))] + [finish]
    for time in range(CHUNKS + len(stages) - 1):
        for k, stage in enumerate(stages):
            if 0 <= time - k < CHUNKS:
                stage(time - k)
    for copy in sends:
        copy.wait_send()


def run_experts(message, stream, w_gate, w_up, w_down):
    n_ep, n_tp = lax.axis_size("ep"), lax.axis_size("tp")
    experts, width, units = w_gate.shape
    row_count = stream.shape[0]
    group = row_count * row_count
    block = n_ep * row_count
    span = width // CHUNKS
    bf16, f32 = jnp.bfloat16, jnp.float32
    vmem = pl.BlockSpec(memory_space=pltpu.VMEM)
    hbm = pl.BlockSpec(memory_space=pl.ANY)
    dma = pltpu.SemaphoreType.DMA
    result = jax.ShapeDtypeStruct((row_count, width), bf16)
    all_rows = n_tp * block
    weight_count = 3 * experts * width * units
    return pl.pallas_call(
        functools.partial(experts_kernel, n_ep, n_tp),
        out_shape=(result, result),
        in_specs=[vmem, vmem, hbm, hbm, hbm],
        out_specs=(vmem, vmem),
        scratch_shapes=[
            pltpu.VMEM((experts, width, units), bf16),
            pltpu.VMEM((experts, width, units), bf16),
            pltpu.VMEM((experts * units, width), bf16),
            pltpu.VMEM((n_tp, n_ep, group, width // row_count + 128), bf16),
            pltpu.VMEM((all_rows, width), bf16),
            pltpu.VMEM((all_rows, experts * units), bf16),
            pltpu.VMEM(((n_tp + 1) // 2, block, width), f32),
            pltpu.VMEM((CHUNKS, n_tp, block, span), bf16),
            pltpu.VMEM((CHUNKS, n_tp, block, span), bf16),
            pltpu.VMEM((CHUNKS, n_ep, group, span // row_count), f32),
            pltpu.VMEM((CHUNKS, n_ep, group, span // row_count), bf16),
            pltpu.VMEM((CHUNKS, n_ep, group, span // row_count), bf16),
            dma((2 * experts + 1,)),
            dma((n_ep,)),
            dma((n_ep,)),
            dma((n_tp, n_ep)),
            dma((n_tp, n_ep)),
            dma((CHUNKS, n_tp)),
            dma((CHUNKS, n_tp)),
            dma((CHUNKS, n_ep)),
            dma((CHUNKS, n_ep)),
        ],
        compiler_params=pltpu.CompilerParams(
            collective_id=0, has_side_effects=True, vmem_limit_bytes=60 * 2**20
        ),
        cost_estimate=pl.CostEstimate(
            flops=2 * all_rows * weight_count, bytes_accessed=2 * weight_count, transcendentals=0
        ),
    )(message, stream, w_gate, w_up, w_down.reshape(experts * units, width))


def local(
    x_rows,
    queries,
    key_cache,
    value_cache,
    new_key,
    new_value,
    lengths,
    norm_gain,
    expert_ids,
    gate_probs,
    expert_place,
    w_gate,
    w_up,
    w_down,
):
    row_count = x_rows.shape[0]
    width = x_rows.shape[1]
    stream = x_rows.astype(jnp.float32) + attend(
        queries, key_cache, value_cache, new_key, new_value, lengths
    )
    scaled = lax.rsqrt(jnp.mean(stream * stream, axis=1, keepdims=True) + 1e-06)
    normed = (stream * scaled * norm_gain.astype(jnp.float32)).astype(jnp.bfloat16)
    experts_total = expert_place.shape[0]
    expert_range = jnp.arange(experts_total, dtype=jnp.int32)
    target = jnp.sum(jnp.where(expert_ids[:, :, None] == expert_range, expert_place, 0), axis=2)
    table = jnp.sum(
        jnp.where(target[:, :, None] == expert_range, gate_probs[:, :, None], 0.0), axis=1
    )
    high = lax.reduce_precision(table, 8, 7)
    middle = lax.reduce_precision(table - high, 8, 7)
    low = table - high - middle
    pieces = jnp.stack([high, middle, low], axis=0).astype(jnp.bfloat16)
    pieces = jnp.pad(pieces, ((0, row_count - 3), (0, 0), (0, 128 - experts_total)))
    quarters = normed.reshape(row_count, row_count, width // row_count).transpose(1, 0, 2)
    message = jnp.concatenate([quarters, pieces], axis=2).reshape(
        row_count * row_count, width // row_count + 128
    )
    return run_experts(message, stream, w_gate, w_up, w_down)


def solution(mesh):
    return jax.shard_map(
        local,
        mesh=mesh,
        in_specs=(
            P(("groups", "ep", "tp"), None),
            P(("groups", "ep", "tp"), None),
            P(("groups", "ep", "tp"), None, None),
            P(("groups", "ep", "tp"), None, None),
            P(("groups", "ep", "tp"), None),
            P(("groups", "ep", "tp"), None),
            P(("groups", "ep", "tp")),
            P(),
            P(("groups", "ep", "tp"), None),
            P(("groups", "ep", "tp"), None),
            P(),
            P("ep", None, "tp"),
            P("ep", None, "tp"),
            P("ep", "tp", None),
        ),
        out_specs=(P(("groups", "ep", "tp"), None), P(("groups", "ep", "tp"), None)),
        check_vma=False,
    )
```

```python
import functools

import jax
import jax.numpy as jnp
from jax import lax
from jax.experimental import pallas as pl
from jax.experimental.pallas import tpu as pltpu
from jax.sharding import PartitionSpec as P

HEAD_DIM = 128
Q_HEADS = 32
KV_HEADS = 2


CHUNKS = 4
MESH = pl.DeviceIdType.MESH


def flip(index, bit):
    return index + bit - 2 * bit * lax.rem(lax.div(index, bit), 2)


def low_bit(number):
    return number & -number


def attend(
    x_ref, query_ref, key_ref, value_ref, new_key_ref, new_value_ref, length_ref, heads, stream
):
    row_count, span = key_ref.shape[0], key_ref.shape[1]
    each = Q_HEADS // KV_HEADS
    factor = HEAD_DIM ** (-0.5)
    for h in range(Q_HEADS):
        heads[:, h, :] = query_ref[:, h * HEAD_DIM : (h + 1) * HEAD_DIM].astype(jnp.float32)
    position = lax.broadcasted_iota(jnp.int32, (each, span), 1)
    for r in range(row_count):
        valid = position < length_ref[r]
        for g in range(KV_HEADS):
            lanes = slice(g * HEAD_DIM, (g + 1) * HEAD_DIM)
            own_rows = slice(g * each, (g + 1) * each)
            query = heads[r, own_rows, :]
            scores = factor * lax.dot_general(
                query.astype(jnp.bfloat16),
                key_ref[r, :, lanes],
                (((1,), (1,)), ((), ())),
                preferred_element_type=jnp.float32,
            )
            fresh_key = new_key_ref[:, lanes].astype(jnp.float32)[r : r + 1]
            fresh_value = new_value_ref[:, lanes].astype(jnp.float32)[r : r + 1]
            own = factor * jnp.sum(query * fresh_key, axis=1, keepdims=True)
            masked = jnp.where(valid, scores, -1e30)
            peak = jnp.maximum(jnp.max(masked, axis=1, keepdims=True), own)
            weight = jnp.where(valid, jnp.exp(masked - peak), 0.0)
            own_weight = jnp.exp(own - peak)
            total = jnp.sum(weight, axis=1, keepdims=True) + own_weight
            coarse = weight.astype(jnp.bfloat16)
            fine = (weight - coarse.astype(jnp.float32)).astype(jnp.bfloat16)
            value = value_ref[r, :, lanes]
            summed = jnp.dot(coarse, value, preferred_element_type=jnp.float32)
            summed = summed + jnp.dot(fine, value, preferred_element_type=jnp.float32)
            heads[r, own_rows, :] = (summed + own_weight * fresh_value) / total
    for h in range(Q_HEADS):
        lanes = slice(h * HEAD_DIM, (h + 1) * HEAD_DIM)
        stream[:, lanes] = x_ref[:, lanes].astype(jnp.float32) + heads[:, h, :]


def pack(stream, gain_ref, ids_ref, prob_ref, place_ref, wide):
    row_count, width = stream.shape
    part = width // row_count
    experts_total = place_ref.shape[1]
    rows = stream[...]
    scaled = lax.rsqrt(jnp.mean(rows * rows, axis=1, keepdims=True) + 1e-06)
    normed = rows * scaled * gain_ref[...].astype(jnp.float32)
    lane = lax.broadcasted_iota(jnp.int32, (row_count, 128), 1)
    ids, probs = ids_ref[...], prob_ref[...]
    table = jnp.zeros((row_count, 128), jnp.float32)
    for k in range(ids.shape[1]):
        table = table + jnp.where(lane == ids[:, k : k + 1], probs[:, k : k + 1], 0.0)
    high = table.astype(jnp.bfloat16).astype(jnp.float32)
    middle = (table - high).astype(jnp.bfloat16).astype(jnp.float32)
    terms = [high, middle, table - high - middle]
    wide[:, part:] = jnp.zeros((row_count * row_count, 128), jnp.float32)
    for q in range(row_count):
        wide[q * row_count : (q + 1) * row_count, :part] = normed[:, q * part : (q + 1) * part]
        if q < len(terms):
            wide[q * row_count : (q + 1) * row_count, part:] = terms[q]
    slot = lax.broadcasted_iota(jnp.int32, (128, experts_total), 0)
    placed = jnp.where(slot == place_ref[...], 1.0, 0.0).astype(jnp.bfloat16)
    wide[:, part:] = lax.dot_general(
        wide[:, part : part + experts_total].astype(jnp.bfloat16),
        placed,
        (((1,), (1,)), ((), ())),
        preferred_element_type=jnp.float32,
    )
    return wide[...].astype(jnp.bfloat16)


def experts_kernel(
    n_ep,
    n_tp,
    x_ref,
    query_ref,
    key_ref,
    value_ref,
    new_key_ref,
    new_value_ref,
    length_ref,
    gain_ref,
    ids_ref,
    prob_ref,
    place_ref,
    w_gate,
    w_up,
    w_down,
    out_ref,
    mix_ref,
    heads,
    stream_ref,
    wide,
    gate_v,
    up_v,
    down_v,
    arrived,
    rows,
    hidden,
    sums,
    sent,
    taken,
    packed_wide,
    packed,
    back,
    weight_sem,
    ep_send,
    ep_recv,
    tp_send,
    tp_recv,
    sum_send,
    sum_recv,
    back_send,
    back_recv,
):
    experts, width, units = gate_v.shape
    row_count = stream_ref.shape[0]
    block = n_ep * row_count
    part = width // row_count
    span = width // CHUNKS
    piece = span // row_count
    bits = []
    bit = n_tp // 2
    while bit:
        bits.append(bit)
        bit //= 2
    me_ep = lax.axis_index("ep")
    me_tp = lax.axis_index("tp")

    loads = []
    for e in range(experts):
        for k, (source, target) in enumerate(((w_gate, gate_v), (w_up, up_v))):
            loads.append(
                pltpu.make_async_copy(source.at[e], target.at[e], weight_sem.at[2 * e + k])
            )
    down_load = pltpu.make_async_copy(w_down, down_v, weight_sem.at[2 * experts])
    for load in loads:
        load.start()
    down_load.start()

    barrier = pltpu.get_barrier_semaphore()
    for j in range(1, n_ep):
        pl.semaphore_signal(
            barrier, inc=1, device_id={"ep": lax.rem(me_ep + j, n_ep)}, device_id_type=MESH
        )
    for b in bits:
        pl.semaphore_signal(barrier, inc=1, device_id={"tp": flip(me_tp, b)}, device_id_type=MESH)
    attend(
        x_ref, query_ref, key_ref, value_ref, new_key_ref, new_value_ref, length_ref, heads, stream_ref
    )
    arrived[0, 0] = pack(stream_ref, gain_ref, ids_ref, prob_ref, place_ref, wide)
    pl.semaphore_wait(barrier, n_ep - 1 + len(bits))

    sends = []
    along = {}
    for j in range(1, n_ep):
        s = n_ep - j
        along[s] = pltpu.make_async_remote_copy(
            src_ref=arrived.at[0, 0],
            dst_ref=arrived.at[0, s],
            send_sem=ep_send.at[s],
            recv_sem=ep_recv.at[s],
            device_id={"ep": lax.rem(me_ep + j, n_ep)},
            device_id_type=MESH,
        )
        along[s].start()
        sends.append(along[s])
    across = {}
    order = [0] + [s for d in range(1, n_ep) for s in (d, n_ep - d) if d <= s]
    order = list(dict.fromkeys(order))
    for m in range(n_tp):
        for s in order:
            if m:
                across[m, s].wait_recv()
            elif s:
                along[s].wait_recv()
            for b in bits:
                if m == 0 or b < low_bit(m):
                    copy = pltpu.make_async_remote_copy(
                        src_ref=arrived.at[m, s],
                        dst_ref=arrived.at[m | b, s],
                        send_sem=tp_send.at[m | b, s],
                        recv_sem=tp_recv.at[m | b, s],
                        device_id={"tp": flip(me_tp, b)},
                        device_id_type=MESH,
                    )
                    copy.start()
                    across[m | b, s] = copy
                    sends.append(copy)

    group = row_count * row_count
    to = lax.broadcasted_iota(jnp.int32, (block, n_ep * group), 0)
    source = lax.broadcasted_iota(jnp.int32, (block, n_ep * group), 1)
    tables = []
    for m in range(n_tp):
        held = arrived[m].reshape(n_ep * group, part + 128)
        table = jnp.zeros((block, 128), jnp.float32)
        for q in range(row_count):
            wanted = lax.div(to, row_count) * group + q * row_count + lax.rem(to, row_count)
            pick = jnp.where(source == wanted, 1.0, 0.0).astype(jnp.bfloat16)
            moved = jnp.dot(pick, held, preferred_element_type=jnp.float32)
            rows[m * block : (m + 1) * block, q * part : (q + 1) * part] = moved[:, :part].astype(
                jnp.bfloat16
            )
            table = table + moved[:, part:]
        tables.append(table)
    table = jnp.concatenate(tables, axis=0)
    lane = lax.broadcasted_iota(jnp.int32, table.shape, 1)

    for e in range(experts):
        loads[2 * e].wait()
        gate = jnp.dot(rows[...], gate_v[e], preferred_element_type=jnp.float32)
        loads[2 * e + 1].wait()
        up = jnp.dot(rows[...], up_v[e], preferred_element_type=jnp.float32)
        share = jnp.sum(
            jnp.where(lane == me_ep * experts + e, table, 0.0), axis=1, keepdims=True
        )
        act = gate / (1.0 + jnp.exp(-gate)) * up * share
        hidden[:, e * units : (e + 1) * units] = act.astype(jnp.bfloat16)
    down_load.wait()

    summing = {}
    returning = {}

    def columns(c):
        return slice(c * span, (c + 1) * span)

    def send_sums(c, b):
        for m in range(1, n_tp):
            if low_bit(m) == b:
                if b > 1:
                    sent[c, m - 1] = sums[m // 2, :, columns(c)].astype(jnp.bfloat16)
                copy = pltpu.make_async_remote_copy(
                    src_ref=sent.at[c, m - 1],
                    dst_ref=taken.at[c, m - 1],
                    send_sem=sum_send.at[c, m],
                    recv_sem=sum_recv.at[c, m],
                    device_id={"tp": flip(me_tp, b)},
                    device_id_type=MESH,
                )
                copy.start()
                summing[c, m] = copy
                sends.append(copy)

    def take_sums(c, b):
        for m in range(1, n_tp):
            if low_bit(m) == b:
                summing[c, m].wait_recv()
                sums[(m - b) // 2, :, columns(c)] += taken[c, m - 1].astype(jnp.float32)

    def send_back(c):
        for s in range(n_ep):
            for q in range(row_count):
                packed_wide[c, s, q * row_count : (q + 1) * row_count, :] = sums[
                    0,
                    s * row_count : (s + 1) * row_count,
                    c * span + q * piece : c * span + (q + 1) * piece,
                ]
            if s:
                packed[c, s] = packed_wide[c, s].astype(jnp.bfloat16)
                copy = pltpu.make_async_remote_copy(
                    src_ref=packed.at[c, s],
                    dst_ref=back.at[c, n_ep - s],
                    send_sem=back_send.at[c, n_ep - s],
                    recv_sem=back_recv.at[c, n_ep - s],
                    device_id={"ep": lax.rem(me_ep + s, n_ep)},
                    device_id_type=MESH,
                )
                copy.start()
                returning[c, s] = copy
                sends.append(copy)

    def compute(c):
        product = jnp.dot(hidden[...], down_v[:, columns(c)], preferred_element_type=jnp.float32)
        for m in range(n_tp):
            mine = product[m * block : (m + 1) * block]
            if m % 2:
                sent[c, m - 1] = mine.astype(jnp.bfloat16)
            else:
                sums[m // 2, :, columns(c)] = mine
        if bits:
            send_sums(c, 1)
        else:
            send_back(c)

    def turn(c, k):
        b = 1 << k
        take_sums(c, b)
        if 2 * b < n_tp:
            send_sums(c, 2 * b)
        else:
            send_back(c)

    def finish(c):
        total = packed_wide[c, 0]
        for s in range(1, n_ep):
            returning[c, s].wait_recv()
            total = total + back[c, n_ep - s].astype(jnp.float32)
        packed_wide[c, 0] = total
        for q in range(row_count):
            place = slice(c * span + q * piece, c * span + (q + 1) * piece)
            mixed = packed_wide[c, 0, q * row_count : (q + 1) * row_count, :]
            mix_ref[:, place] = mixed
            out_ref[:, place] = stream_ref[:, place] + mixed

    stages = [compute] + [functools.partial(turn, k=k) for k in range(len(bits))] + [finish]
    for time in range(CHUNKS + len(stages) - 1):
        for k, stage in enumerate(stages):
            if 0 <= time - k < CHUNKS:
                stage(time - k)
    for copy in sends:
        copy.wait_send()


def local(
    x_rows,
    queries,
    key_cache,
    value_cache,
    new_key,
    new_value,
    lengths,
    norm_gain,
    expert_ids,
    gate_probs,
    expert_place,
    w_gate,
    w_up,
    w_down,
):
    n_ep, n_tp = lax.axis_size("ep"), lax.axis_size("tp")
    experts, width, units = w_gate.shape
    row_count = x_rows.shape[0]
    group = row_count * row_count
    block = n_ep * row_count
    span = width // CHUNKS
    bf16, f32 = jnp.bfloat16, jnp.float32
    vmem = pl.BlockSpec(memory_space=pltpu.VMEM)
    hbm = pl.BlockSpec(memory_space=pl.ANY)
    dma = pltpu.SemaphoreType.DMA
    smem = pl.BlockSpec(memory_space=pltpu.SMEM)
    result = jax.ShapeDtypeStruct((row_count, width), f32)
    all_rows = n_tp * block
    weight_count = 3 * experts * width * units
    layer_out, mixed = pl.pallas_call(
        functools.partial(experts_kernel, n_ep, n_tp),
        out_shape=(result, result),
        in_specs=[vmem] * 6 + [smem] + [vmem] * 4 + [hbm] * 3,
        out_specs=(vmem, vmem),
        scratch_shapes=[
            pltpu.VMEM((row_count, Q_HEADS, HEAD_DIM), f32),
            pltpu.VMEM((row_count, width), f32),
            pltpu.VMEM((group, width // row_count + 128), f32),
            pltpu.VMEM((experts, width, units), bf16),
            pltpu.VMEM((experts, width, units), bf16),
            pltpu.VMEM((experts * units, width), bf16),
            pltpu.VMEM((n_tp, n_ep, group, width // row_count + 128), bf16),
            pltpu.VMEM((all_rows, width), bf16),
            pltpu.VMEM((all_rows, experts * units), bf16),
            pltpu.VMEM(((n_tp + 1) // 2, block, width), f32),
            pltpu.VMEM((CHUNKS, max(n_tp - 1, 1), block, span), bf16),
            pltpu.VMEM((CHUNKS, max(n_tp - 1, 1), block, span), bf16),
            pltpu.VMEM((CHUNKS, n_ep, group, span // row_count), f32),
            pltpu.VMEM((CHUNKS, n_ep, group, span // row_count), bf16),
            pltpu.VMEM((CHUNKS, n_ep, group, span // row_count), bf16),
            dma((2 * experts + 1,)),
            dma((n_ep,)),
            dma((n_ep,)),
            dma((n_tp, n_ep)),
            dma((n_tp, n_ep)),
            dma((CHUNKS, n_tp)),
            dma((CHUNKS, n_tp)),
            dma((CHUNKS, n_ep)),
            dma((CHUNKS, n_ep)),
        ],
        compiler_params=pltpu.CompilerParams(
            collective_id=0, has_side_effects=True, vmem_limit_bytes=60 * 2**20
        ),
        cost_estimate=pl.CostEstimate(
            flops=2 * all_rows * weight_count, bytes_accessed=2 * weight_count, transcendentals=0
        ),
    )(
        x_rows,
        queries,
        key_cache,
        value_cache,
        new_key,
        new_value,
        lengths,
        norm_gain.reshape(1, width),
        expert_ids,
        gate_probs,
        expert_place.reshape(1, -1),
        w_gate,
        w_up,
        w_down.reshape(experts * units, width),
    )
    return layer_out.astype(bf16), mixed.astype(bf16)


def solution(mesh):
    return jax.shard_map(
        local,
        mesh=mesh,
        in_specs=(
            P(("groups", "ep", "tp"), None),
            P(("groups", "ep", "tp"), None),
            P(("groups", "ep", "tp"), None, None),
            P(("groups", "ep", "tp"), None, None),
            P(("groups", "ep", "tp"), None),
            P(("groups", "ep", "tp"), None),
            P(("groups", "ep", "tp")),
            P(),
            P(("groups", "ep", "tp"), None),
            P(("groups", "ep", "tp"), None),
            P(),
            P("ep", None, "tp"),
            P("ep", None, "tp"),
            P("ep", "tp", None),
        ),
        out_specs=(P(("groups", "ep", "tp"), None), P(("groups", "ep", "tp"), None)),
        check_vma=False,
    )
```

```python
import functools

import jax
import jax.numpy as jnp
from jax import lax
from jax.experimental import pallas as pl
from jax.experimental.pallas import tpu as pltpu
from jax.sharding import PartitionSpec as P

HEAD_DIM = 128
Q_HEADS = 32
KV_HEADS = 2


CHUNKS = 4
MESH = pl.DeviceIdType.MESH


def flip(index, bit):
    return index + bit - 2 * bit * lax.rem(lax.div(index, bit), 2)


def low_bit(number):
    return number & -number


def attend(
    x_ref, query_ref, key_ref, value_ref, new_key_ref, new_value_ref, length_ref, heads, stream
):
    row_count, span = key_ref.shape[0], key_ref.shape[1]
    each = Q_HEADS // KV_HEADS
    factor = HEAD_DIM ** (-0.5)
    for h in range(Q_HEADS):
        heads[:, h, :] = query_ref[:, h * HEAD_DIM : (h + 1) * HEAD_DIM].astype(jnp.float32)
    position = lax.broadcasted_iota(jnp.int32, (each, span), 1)
    for r in range(row_count):
        valid = position < length_ref[r]
        for g in range(KV_HEADS):
            lanes = slice(g * HEAD_DIM, (g + 1) * HEAD_DIM)
            own_rows = slice(g * each, (g + 1) * each)
            query = heads[r, own_rows, :]
            scores = factor * lax.dot_general(
                query.astype(jnp.bfloat16),
                key_ref[r, :, lanes],
                (((1,), (1,)), ((), ())),
                preferred_element_type=jnp.float32,
            )
            fresh_key = new_key_ref[:, lanes].astype(jnp.float32)[r : r + 1]
            fresh_value = new_value_ref[:, lanes].astype(jnp.float32)[r : r + 1]
            own = factor * jnp.sum(query * fresh_key, axis=1, keepdims=True)
            masked = jnp.where(valid, scores, -1e30)
            peak = jnp.maximum(jnp.max(masked, axis=1, keepdims=True), own)
            weight = jnp.where(valid, jnp.exp(masked - peak), 0.0)
            own_weight = jnp.exp(own - peak)
            total = jnp.sum(weight, axis=1, keepdims=True) + own_weight
            coarse = weight.astype(jnp.bfloat16)
            fine = (weight - coarse.astype(jnp.float32)).astype(jnp.bfloat16)
            value = value_ref[r, :, lanes]
            summed = jnp.dot(coarse, value, preferred_element_type=jnp.float32)
            summed = summed + jnp.dot(fine, value, preferred_element_type=jnp.float32)
            heads[r, own_rows, :] = (summed + own_weight * fresh_value) / total
    for h in range(Q_HEADS):
        lanes = slice(h * HEAD_DIM, (h + 1) * HEAD_DIM)
        stream[:, lanes] = x_ref[:, lanes].astype(jnp.float32) + heads[:, h, :]


def pack(stream, gain_ref, ids_ref, prob_ref, place_ref, wide):
    row_count, width = stream.shape
    part = width // row_count
    experts_total = place_ref.shape[1]
    rows = stream[...]
    scaled = lax.rsqrt(jnp.mean(rows * rows, axis=1, keepdims=True) + 1e-06)
    normed = rows * scaled * gain_ref[...].astype(jnp.float32).reshape(1, width)
    lane = lax.broadcasted_iota(jnp.int32, (row_count, 128), 1)
    ids, probs = ids_ref[...], prob_ref[...]
    table = jnp.zeros((row_count, 128), jnp.float32)
    for k in range(ids.shape[1]):
        table = table + jnp.where(lane == ids[:, k : k + 1], probs[:, k : k + 1], 0.0)
    high = table.astype(jnp.bfloat16).astype(jnp.float32)
    middle = (table - high).astype(jnp.bfloat16).astype(jnp.float32)
    terms = [high, middle, table - high - middle]
    wide[:, part:] = jnp.zeros((row_count * row_count, 128), jnp.float32)
    for q in range(row_count):
        wide[q * row_count : (q + 1) * row_count, :part] = normed[:, q * part : (q + 1) * part]
        if q < len(terms):
            wide[q * row_count : (q + 1) * row_count, part:] = terms[q]
    slot = lax.broadcasted_iota(jnp.int32, (128, experts_total), 0)
    placed = jnp.where(slot == place_ref[...], 1.0, 0.0).astype(jnp.bfloat16)
    wide[:, part:] = lax.dot_general(
        wide[:, part : part + experts_total].astype(jnp.bfloat16),
        placed,
        (((1,), (1,)), ((), ())),
        preferred_element_type=jnp.float32,
    )
    return wide[...].astype(jnp.bfloat16)


def experts_kernel(
    n_ep,
    n_tp,
    x_ref,
    query_ref,
    key_ref,
    value_ref,
    new_key_ref,
    new_value_ref,
    length_ref,
    gain_ref,
    ids_ref,
    prob_ref,
    place_ref,
    w_gate,
    w_up,
    w_down,
    out_ref,
    mix_ref,
    heads,
    stream_ref,
    wide,
    gate_v,
    up_v,
    down_v,
    arrived,
    rows,
    hidden,
    sums,
    sent,
    taken,
    packed_wide,
    packed,
    back,
    weight_sem,
    ep_send,
    ep_recv,
    tp_send,
    tp_recv,
    sum_send,
    sum_recv,
    back_send,
    back_recv,
):
    experts, width, units = gate_v.shape
    row_count = stream_ref.shape[0]
    block = n_ep * row_count
    part = width // row_count
    span = width // CHUNKS
    piece = span // row_count
    bits = []
    bit = n_tp // 2
    while bit:
        bits.append(bit)
        bit //= 2
    me_ep = lax.axis_index("ep")
    me_tp = lax.axis_index("tp")

    loads = []
    for e in range(experts):
        for k, (source, target) in enumerate(((w_gate, gate_v), (w_up, up_v))):
            loads.append(
                pltpu.make_async_copy(source.at[e], target.at[e], weight_sem.at[2 * e + k])
            )
    down_load = pltpu.make_async_copy(w_down, down_v, weight_sem.at[2 * experts])
    for load in loads:
        load.start()

    barrier = pltpu.get_barrier_semaphore()
    for j in range(1, n_ep):
        pl.semaphore_signal(
            barrier, inc=1, device_id={"ep": lax.rem(me_ep + j, n_ep)}, device_id_type=MESH
        )
    for b in bits:
        pl.semaphore_signal(barrier, inc=1, device_id={"tp": flip(me_tp, b)}, device_id_type=MESH)
    attend(
        x_ref, query_ref, key_ref, value_ref, new_key_ref, new_value_ref, length_ref, heads, stream_ref
    )
    arrived[0, 0] = pack(stream_ref, gain_ref, ids_ref, prob_ref, place_ref, wide)
    pl.semaphore_wait(barrier, n_ep - 1 + len(bits))

    sends = []
    along = {}
    for j in range(1, n_ep):
        s = n_ep - j
        along[s] = pltpu.make_async_remote_copy(
            src_ref=arrived.at[0, 0],
            dst_ref=arrived.at[0, s],
            send_sem=ep_send.at[s],
            recv_sem=ep_recv.at[s],
            device_id={"ep": lax.rem(me_ep + j, n_ep)},
            device_id_type=MESH,
        )
        along[s].start()
        sends.append(along[s])
    across = {}
    order = [0] + [s for d in range(1, n_ep) for s in (d, n_ep - d) if d <= s]
    order = list(dict.fromkeys(order))
    for m in range(n_tp):
        for s in order:
            if m:
                across[m, s].wait_recv()
            elif s:
                along[s].wait_recv()
            for b in bits:
                if m == 0 or b < low_bit(m):
                    copy = pltpu.make_async_remote_copy(
                        src_ref=arrived.at[m, s],
                        dst_ref=arrived.at[m | b, s],
                        send_sem=tp_send.at[m | b, s],
                        recv_sem=tp_recv.at[m | b, s],
                        device_id={"tp": flip(me_tp, b)},
                        device_id_type=MESH,
                    )
                    copy.start()
                    across[m | b, s] = copy
                    sends.append(copy)
    down_load.start()

    group = row_count * row_count
    to = lax.broadcasted_iota(jnp.int32, (block, n_ep * group), 0)
    source = lax.broadcasted_iota(jnp.int32, (block, n_ep * group), 1)
    tables = []
    for m in range(n_tp):
        held = arrived[m].reshape(n_ep * group, part + 128)
        table = jnp.zeros((block, 128), jnp.float32)
        for q in range(row_count):
            wanted = lax.div(to, row_count) * group + q * row_count + lax.rem(to, row_count)
            pick = jnp.where(source == wanted, 1.0, 0.0).astype(jnp.bfloat16)
            moved = jnp.dot(pick, held, preferred_element_type=jnp.float32)
            rows[m * block : (m + 1) * block, q * part : (q + 1) * part] = moved[:, :part].astype(
                jnp.bfloat16
            )
            table = table + moved[:, part:]
        tables.append(table)
    table = jnp.concatenate(tables, axis=0)
    lane = lax.broadcasted_iota(jnp.int32, table.shape, 1)

    for e in range(experts):
        loads[2 * e].wait()
        gate = jnp.dot(rows[...], gate_v[e], preferred_element_type=jnp.float32)
        loads[2 * e + 1].wait()
        up = jnp.dot(rows[...], up_v[e], preferred_element_type=jnp.float32)
        share = jnp.sum(
            jnp.where(lane == me_ep * experts + e, table, 0.0), axis=1, keepdims=True
        )
        act = gate / (1.0 + jnp.exp(-gate)) * up * share
        hidden[:, e * units : (e + 1) * units] = act.astype(jnp.bfloat16)
    down_load.wait()

    summing = {}
    returning = {}

    def columns(c):
        return slice(c * span, (c + 1) * span)

    def send_sums(c, b):
        for m in range(1, n_tp):
            if low_bit(m) == b:
                if b > 1:
                    sent[c, m - 1] = sums[m // 2, :, columns(c)].astype(jnp.bfloat16)
                copy = pltpu.make_async_remote_copy(
                    src_ref=sent.at[c, m - 1],
                    dst_ref=taken.at[c, m - 1],
                    send_sem=sum_send.at[c, m],
                    recv_sem=sum_recv.at[c, m],
                    device_id={"tp": flip(me_tp, b)},
                    device_id_type=MESH,
                )
                copy.start()
                summing[c, m] = copy
                sends.append(copy)

    def take_sums(c, b):
        for m in range(1, n_tp):
            if low_bit(m) == b:
                summing[c, m].wait_recv()
                sums[(m - b) // 2, :, columns(c)] += taken[c, m - 1].astype(jnp.float32)

    def send_back(c):
        for s in range(n_ep):
            for q in range(row_count):
                packed_wide[c, s, q * row_count : (q + 1) * row_count, :] = sums[
                    0,
                    s * row_count : (s + 1) * row_count,
                    c * span + q * piece : c * span + (q + 1) * piece,
                ]
            if s:
                packed[c, s] = packed_wide[c, s].astype(jnp.bfloat16)
                copy = pltpu.make_async_remote_copy(
                    src_ref=packed.at[c, s],
                    dst_ref=back.at[c, n_ep - s],
                    send_sem=back_send.at[c, n_ep - s],
                    recv_sem=back_recv.at[c, n_ep - s],
                    device_id={"ep": lax.rem(me_ep + s, n_ep)},
                    device_id_type=MESH,
                )
                copy.start()
                returning[c, s] = copy
                sends.append(copy)

    def compute(c):
        product = jnp.dot(hidden[...], down_v[:, columns(c)], preferred_element_type=jnp.float32)
        for m in range(n_tp):
            mine = product[m * block : (m + 1) * block]
            if m % 2:
                sent[c, m - 1] = mine.astype(jnp.bfloat16)
            else:
                sums[m // 2, :, columns(c)] = mine
        if bits:
            send_sums(c, 1)
        else:
            send_back(c)

    def turn(c, k):
        b = 1 << k
        take_sums(c, b)
        if 2 * b < n_tp:
            send_sums(c, 2 * b)
        else:
            send_back(c)

    def finish(c):
        total = packed_wide[c, 0]
        for s in range(1, n_ep):
            returning[c, s].wait_recv()
            total = total + back[c, n_ep - s].astype(jnp.float32)
        packed_wide[c, 0] = total
        for q in range(row_count):
            place = slice(c * span + q * piece, c * span + (q + 1) * piece)
            mixed = packed_wide[c, 0, q * row_count : (q + 1) * row_count, :]
            mix_ref[:, place] = mixed
            out_ref[:, place] = stream_ref[:, place]

    stages = [compute] + [functools.partial(turn, k=k) for k in range(len(bits))] + [finish]
    for time in range(CHUNKS + len(stages) - 1):
        for k, stage in enumerate(stages):
            if 0 <= time - k < CHUNKS:
                stage(time - k)
    for copy in sends:
        copy.wait_send()


def local(
    x_rows,
    queries,
    key_cache,
    value_cache,
    new_key,
    new_value,
    lengths,
    norm_gain,
    expert_ids,
    gate_probs,
    expert_place,
    w_gate,
    w_up,
    w_down,
):
    n_ep, n_tp = lax.axis_size("ep"), lax.axis_size("tp")
    experts, width, units = w_gate.shape
    row_count = x_rows.shape[0]
    group = row_count * row_count
    block = n_ep * row_count
    span = width // CHUNKS
    bf16, f32 = jnp.bfloat16, jnp.float32
    vmem = pl.BlockSpec(memory_space=pltpu.VMEM)
    hbm = pl.BlockSpec(memory_space=pl.ANY)
    dma = pltpu.SemaphoreType.DMA
    smem = pl.BlockSpec(memory_space=pltpu.SMEM)
    result = jax.ShapeDtypeStruct((row_count, width), f32)
    all_rows = n_tp * block
    weight_count = 3 * experts * width * units
    stream, mixed = pl.pallas_call(
        functools.partial(experts_kernel, n_ep, n_tp),
        out_shape=(result, result),
        in_specs=[vmem] * 6 + [smem] + [vmem] * 4 + [hbm] * 3,
        out_specs=(vmem, vmem),
        scratch_shapes=[
            pltpu.VMEM((row_count, Q_HEADS, HEAD_DIM), f32),
            pltpu.VMEM((row_count, width), f32),
            pltpu.VMEM((group, width // row_count + 128), f32),
            pltpu.VMEM((experts, width, units), bf16),
            pltpu.VMEM((experts, width, units), bf16),
            pltpu.VMEM((experts * units, width), bf16),
            pltpu.VMEM((n_tp, n_ep, group, width // row_count + 128), bf16),
            pltpu.VMEM((all_rows, width), bf16),
            pltpu.VMEM((all_rows, experts * units), bf16),
            pltpu.VMEM(((n_tp + 1) // 2, block, width), f32),
            pltpu.VMEM((CHUNKS, max(n_tp - 1, 1), block, span), bf16),
            pltpu.VMEM((CHUNKS, max(n_tp - 1, 1), block, span), bf16),
            pltpu.VMEM((CHUNKS, n_ep, group, span // row_count), f32),
            pltpu.VMEM((CHUNKS, n_ep, group, span // row_count), bf16),
            pltpu.VMEM((CHUNKS, n_ep, group, span // row_count), bf16),
            dma((2 * experts + 1,)),
            dma((n_ep,)),
            dma((n_ep,)),
            dma((n_tp, n_ep)),
            dma((n_tp, n_ep)),
            dma((CHUNKS, n_tp)),
            dma((CHUNKS, n_tp)),
            dma((CHUNKS, n_ep)),
            dma((CHUNKS, n_ep)),
        ],
        compiler_params=pltpu.CompilerParams(
            collective_id=0, has_side_effects=True, vmem_limit_bytes=60 * 2**20
        ),
        cost_estimate=pl.CostEstimate(
            flops=2 * all_rows * weight_count, bytes_accessed=2 * weight_count, transcendentals=0
        ),
    )(
        x_rows,
        queries,
        key_cache,
        value_cache,
        new_key,
        new_value,
        lengths,
        norm_gain,
        expert_ids,
        gate_probs,
        expert_place.reshape(1, -1),
        w_gate,
        w_up,
        w_down.reshape(experts * units, width),
    )
    return (stream + mixed).astype(bf16), mixed.astype(bf16)


def solution(mesh):
    return jax.shard_map(
        local,
        mesh=mesh,
        in_specs=(
            P(("groups", "ep", "tp"), None),
            P(("groups", "ep", "tp"), None),
            P(("groups", "ep", "tp"), None, None),
            P(("groups", "ep", "tp"), None, None),
            P(("groups", "ep", "tp"), None),
            P(("groups", "ep", "tp"), None),
            P(("groups", "ep", "tp")),
            P(),
            P(("groups", "ep", "tp"), None),
            P(("groups", "ep", "tp"), None),
            P(),
            P("ep", None, "tp"),
            P("ep", None, "tp"),
            P("ep", "tp", None),
        ),
        out_specs=(P(("groups", "ep", "tp"), None), P(("groups", "ep", "tp"), None)),
        check_vma=False,
    )
```
